512 devices in a mesh: prow: 16 (over y, core), pcol: 32 (over x, z).
Axes of the slice: x: 4, y: 8, z: 8, core: 2. Of those that a mesh axis runs over, the one named last changes fastest.
Arguments:
- trailing: float32 [8, 16, 128, 4, 32, 128], P(None, 'prow', None, None, 'pcol'), may hold values from -8 to 8, as said below
- reflectors: float32 [8, 16, 128, 256], P(None, 'prow', None, 'pcol'), may hold values from -0.3125 to 0.3125
- tfactor: float32 [256, 256], replicated, may hold values from -0.375 to 0.375
Outputs:
- updated: float32 [8, 16, 128, 4, 32, 128], P(None, 'prow', None, None, 'pcol')
The draws below stay inside these ranges and needn't reach their ends.
Inputs may be any that keep to these rules, and one draw needn't show every extreme that they name: trailing is symmetric as a matrix of order 16384.
All inputs are finite; a program needn't handle non-finite values.
Results may differ from the reference program's by a relative error of at most 0.00011.
Values sent between devices are 32-bit elements; how exact they have to be, the bound alone decides.
A program may use at most 64 MiB of HBM per device.

```python
import jax
import jax.numpy as jnp
from jax import lax

TILE = 128
NB = 256
RT = 8
CT = 4
ORDER = 16384
N_PROW = 16


def draw_trailing(key, part):
    key = jax.random.fold_in(key, 11)
    base = jnp.clip(jax.random.normal(key, (ORDER, ORDER), jnp.float32), -5.5, 5.5)
    symmetric = (base + base.T) * 0.70710678
    return symmetric.reshape(RT, ORDER // (RT * TILE), TILE, CT, ORDER // (CT * TILE), TILE)


def block_scale(key, shape, split, smallest, high):
    def one(axis_at, blocks):
        heights = jax.random.uniform(jax.random.fold_in(jax.random.fold_in(key, 6), axis_at), (blocks,), jnp.float32, smallest / len(split), high / len(split))
        return jnp.repeat(jnp.exp(heights), shape[axis_at] // blocks).reshape((-1,) + (1,) * (len(shape) - axis_at - 1))

    level = one(*split[0])
    for cut in split[1:]:
        level = level * one(*cut)
    return level


def centred(rng, dims, width, most, cuts=(), dtype=jnp.bfloat16):
    values = jax.random.normal(rng, dims, jnp.float32) * width
    if len(cuts) > 0:
        values = block_scale(rng, dims, cuts, -0.22, 0.18) * values
    return jnp.clip(values, min=-most, max=most).astype(dtype)


def setup_inputs(seed: int = 0) -> dict:
    splits = jax.random.split(jax.random.key(seed), 4)
    return {
        "trailing": draw_trailing(jax.random.fold_in(splits[3], 71), 0),
        "reflectors": centred(splits[1], (RT, N_PROW, TILE, NB), ((NB * ORDER) ** -0.25), 0.3125, ((1, 16), (3, 32)), jnp.float32),
        "tfactor": centred(splits[2], (NB, NB), NB ** -0.5, 0.375, (), jnp.float32),
    }


def matmul(left, right):
    return jnp.dot(left, right, precision=lax.Precision.HIGHEST, preferred_element_type=jnp.float32)


def reference(trailing, reflectors, tfactor):
    order_size = trailing.shape[0] * trailing.shape[1] * trailing.shape[2]
    full_matrix = trailing.reshape(order_size, order_size)
    vectors = reflectors.reshape(order_size, reflectors.shape[3])
    product = matmul(full_matrix, vectors)
    w_first = matmul(product, tfactor)
    inner_sum = matmul(vectors.T, w_first)
    correction = matmul(tfactor.T, inner_sum)
    w_full = w_first - 0.5 * matmul(vectors, correction)
    result = full_matrix - matmul(vectors, w_full.T) - matmul(w_full, vectors.T)
    return result.reshape(trailing.shape)
```

```python
import types

import jax
import jax.numpy as jnp
from jax import lax
from jax.experimental import pallas as pl
from jax.experimental.pallas import tpu as pltpu
from jax.sharding import PartitionSpec as P

F32 = jnp.float32
BF16 = jnp.bfloat16
MESH = pl.DeviceIdType.MESH
NX, NY, NZ, NC = 4, 8, 8, 2
RING = (1, 7, 2, 6, 3, 5, 4)


def wrap(value, size):
    return lax.rem(value + 2 * size, size)


def device(x, y, z, c):
    return (y * NC + c, x * NZ + z)


def split(value):
    high = value.astype(BF16)
    return high, (value - high.astype(F32)).astype(BF16)


def dot3(left, right, dims=((1,), (0,))):
    def one(a, b):
        return lax.dot_general(a, b, (dims, ((), ())), preferred_element_type=F32)

    return one(left[0], right[0]) + (one(left[0], right[1]) + one(left[1], right[0]))


def copy_to(src, dst, send, recv, target):
    return pltpu.make_async_remote_copy(
        src_ref=src, dst_ref=dst, send_sem=send, recv_sem=recv, device_id=target, device_id_type=MESH
    )


def kernel(
    yt_hbm, a_hbm, t_hbm, o_hbm,
    a_f32, a_hi, a_lo, t_f32, out,
    yr, yt_hi, yt_lo, yr_hi, yr_lo, yc, zt_hi, zt_lo, zt_f32,
    q_all, q_in, q_sum, r_in, gc, gr,
    n_own, n_z, n_zsum, n_x, n_all,
    local, o_sem,
    yz_s, yz_r, yx_s, yx_r, yv_s, yv_r,
    gz_s, gz_r, gx_s, gx_r, gv_s, gv_r,
    c1_s, c1_r, c2_s, c2_r, c3_s, c3_r,
    q_s, q_r, r_s, r_r, p_s, p_r, cy_s, cy_r, cc_s, cc_r,
    nz_s, nz_r, nx_s, nx_r, ny_s, ny_r, nc_s, nc_r,
):
    row, col = lax.axis_index("prow"), lax.axis_index("pcol")
    y, c = lax.div(row, NC), lax.rem(row, NC)
    x, z = lax.div(col, NZ), lax.rem(col, NZ)
    other = 1 - c
    sends = []

    def send(src, dst, send_sem, recv_sem, target):
        copy = copy_to(src, dst, send_sem, recv_sem, target)
        copy.start()
        sends.append(copy)

    def arrived(dst, send_sem, recv_sem, target):
        copy_to(dst, dst, send_sem, recv_sem, target).wait_recv()

    at_z = lambda d: device(x, y, wrap(z + d, NZ), c)
    at_x = lambda d: device(wrap(x + d, NX), y, z, c)
    at_y = lambda d: device(x, wrap(y + d, NY), z, c)
    at_c = device(x, y, z, other)

    row_x, row_z = lax.div(y, 4), 2 * lax.rem(y, 4) + c
    col_y, col_c = lax.rem(x, 2) * 4 + lax.div(z, 2), lax.rem(z, 2)

    mirror_y = wrap(y + z - row_z + 4, NY)
    mirror_dx = [wrap(x - row_x - 2 * s, NX) for s in range(2)]
    mirror_to = [device(row_x + 2 * s, mirror_y, row_z, lax.rem(mirror_dx[s], 2)) for s in range(2)]
    from_z = wrap(z + y - col_y + 4, NZ)
    from_x = [wrap(x + c + 2 * m, NX) for m in range(2)]
    mirror_from = [device(from_x[m], col_y, from_z, col_c) for m in range(2)]
    piece_to = device(wrap(x + c, NX), col_y, from_z, col_c)
    src_c = wrap(x - row_x, 2)
    src_x = wrap(x - src_c, NX)
    piece_from = device(src_x, mirror_y, row_z, src_c)

    barrier = pltpu.get_barrier_semaphore()
    greeted = [at_z(d) for d in RING] + [at_y(d) for d in RING] + [at_x(d) for d in (1, 2, 3)] + [at_c]
    greeted += mirror_to + mirror_from + [piece_to, piece_from]
    for peer in greeted:
        pl.semaphore_signal(barrier, inc=1, device_id=peer, device_id_type=MESH)

    y_in = pltpu.make_async_copy(yt_hbm, yr.at[x, z], local.at[0])
    a_in = pltpu.make_async_copy(a_hbm, a_f32, local.at[1])
    t_in = pltpu.make_async_copy(t_hbm, t_f32, local.at[2])
    y_in.start()
    a_in.start()
    t_in.start()
    y_in.wait()
    pl.semaphore_wait(barrier, len(greeted))

    def gather_begin(buf, slot, sems):
        own = buf.at[slot(0, 0)]
        for way, dx in ((0, 1), (1, -1)):
            send(own, own, sems.xs.at[way, 0], sems.xr.at[way, 0], at_x(dx))
        for i, d in enumerate(RING):
            send(own, own, sems.zs.at[i], sems.zr.at[i], at_z(d))

    def gather_z(buf, slot, sems, i):
        d = RING[i]
        block = buf.at[slot(0, -d)]
        arrived(block, sems.zs.at[i], sems.zr.at[i], at_z(-d))
        for way, dx in ((0, 1), (1, -1)):
            send(block, block, sems.xs.at[way, i + 1], sems.xr.at[way, i + 1], at_x(dx))

    def gather_x(buf, slot, sems, i):
        d = (0,) + RING
        for way, dx in ((0, 1), (1, -1)):
            block = buf.at[slot(-dx, -d[i])]
            arrived(block, sems.xs.at[way, i], sems.xr.at[way, i], at_x(-dx))
            if i % 2 == way:
                send(block, block, sems.vs.at[i], sems.vr.at[i], at_x(dx))

    def gather_end(buf, slot, sems, i):
        d = (0,) + RING
        dx = 1 if i % 2 == 0 else -1
        block = buf.at[slot(2, -d[i])]
        arrived(block, sems.vs.at[i], sems.vr.at[i], at_x(-dx))

    y_sems = types.SimpleNamespace(zs=yz_s, zr=yz_r, xs=yx_s, xr=yx_r, vs=yv_s, vr=yv_r)
    g_sems = types.SimpleNamespace(zs=gz_s, zr=gz_r, xs=gx_s, xr=gx_r, vs=gv_s, vr=gv_r)

    def y_slot(dx, dz):
        return (wrap(x + dx, NX), wrap(z + dz, NZ))

    def g_slot(dx, dz):
        at = wrap(x + dx, NX)
        part = wrap(at - row_x, 2)
        return (2 * lax.div(wrap(at - part, NX), 2) + part, wrap(y + z + dz - row_z + 4, NY))

    gather_begin(yr, y_slot, y_sems)
    for s in range(2):
        m = lax.div(mirror_dx[s], 2)
        send(yr.at[x, z, :, s], yc.at[x, z], c1_s.at[s], c1_r.at[m], mirror_to[s])

    a_in.wait()
    for tile in range(8):
        for b in range(4):
            high, low = split(a_f32[pl.ds(tile * 512 + b, 128, stride=4), :])
            a_hi[tile * 128 : tile * 128 + 128, b * 128 : b * 128 + 128] = high
            a_lo[tile * 128 : tile * 128 + 128, b * 128 : b * 128 + 128] = low

    for i in range(7):
        gather_z(yr, y_slot, y_sems, i)
        if i >= 2:
            gather_x(yr, y_slot, y_sems, i - 2)
    for m in range(2):
        block = yc.at[from_x[m], from_z]
        arrived(block, c1_s.at[m], c1_r.at[m], mirror_from[m])
        for i, d in enumerate(RING):
            send(block, block, c2_s.at[m, i], c2_r.at[m, i], at_y(d))
    for i in range(5, 8):
        gather_x(yr, y_slot, y_sems, i)
    for i in range(8):
        gather_end(yr, y_slot, y_sems, i)

    for tile in range(8):
        high, low = split(yr[:, :, tile // 2, tile % 2].reshape(256, 128))
        yt_hi[:, tile * 128 : tile * 128 + 128] = high
        yt_lo[:, tile * 128 : tile * 128 + 128] = low
    for half in range(2):
        cols = slice(half * 256, half * 256 + 256)
        part = dot3((yt_hi[...], yt_lo[...]), (a_hi[:, cols], a_lo[:, cols]))
        for k in range(2):
            q_all[:, :, :, half * 2 + k] = part[:, k * 128 : k * 128 + 128].reshape(2, 8, 2, 8, 128)
    send(q_all.at[other], q_in, q_s.at[0], q_r.at[0], at_c)

    for m in range(2):
        for i, d in enumerate(RING):
            block = yc.at[from_x[m], wrap(from_z - d, NZ)]
            arrived(block, c2_s.at[m, i], c2_r.at[m, i], at_y(-d))
        send(yc.at[from_x[m]], yc.at[from_x[m]], c3_s.at[m], c3_r.at[m], at_c)

    arrived(q_in, q_s.at[0], q_r.at[0], at_c)
    for i, d in enumerate(RING):
        to = wrap(y + d, NY)
        q_sum[to] = q_all[c, to] + q_in[to]
        send(q_sum.at[to], r_in.at[i], r_s.at[i], r_r.at[i], at_y(d))
    q_sum[y] = q_all[c, y] + q_in[y]

    for m in range(2):
        block = yc.at[wrap(x + other + 2 * m, NX)]
        arrived(block, c3_s.at[m], c3_r.at[m], at_c)
    t_in.wait()
    for b in range(4):
        rhs = split(yc[:, :, b].reshape(256, 128))
        part = dot3(split(t_f32[...]), rhs)
        zt_f32[:, b * 128 : b * 128 + 128] = part
        high, low = split(part)
        zt_hi[:, b * 128 : b * 128 + 128] = high
        zt_lo[:, b * 128 : b * 128 + 128] = low
    for tile in range(8):
        high, low = split(yr[:, :, tile // 2, tile % 2].reshape(256, 128).T)
        yr_hi[tile * 128 : tile * 128 + 128, :] = high
        yr_lo[tile * 128 : tile * 128 + 128, :] = low

    total = q_sum[y]
    for i, d in enumerate(RING):
        arrived(r_in.at[i], r_s.at[i], r_r.at[i], at_y(-d))
        total = total + r_in[i]
    gc[c, y] = total

    own = gc.at[c, y]
    send(own, gr.at[2 * lax.div(x, 2) + c, y], p_s.at[0], p_r.at[0], piece_to)
    for i, d in enumerate(RING):
        send(own, own, cy_s.at[i], cy_r.at[i], at_y(d))
    part = jnp.zeros((16, 256), F32)
    for b in range(4):
        part = part + dot3(
            split(total[:, b].reshape(16, 128)), split(yc[:, :, b].reshape(256, 128)), ((1,), (1,))
        )
    n_own[...] = part
    for i, d in enumerate(RING):
        send(n_own, n_z.at[i], nz_s.at[i], nz_r.at[i], at_z(d))

    arrived(gr.at[g_slot(0, 0)], p_s.at[0], p_r.at[0], piece_from)
    gather_begin(gr, g_slot, g_sems)

    part = n_own[...]
    for i, d in enumerate(RING):
        arrived(n_z.at[i], nz_s.at[i], nz_r.at[i], at_z(-d))
        part = part + n_z[i]
    n_zsum[...] = part
    for i in range(3):
        send(n_zsum, n_x.at[i], nx_s.at[i], nx_r.at[i], at_x(i + 1))

    for i in range(4):
        gather_z(gr, g_slot, g_sems, i)
    for i in range(3):
        arrived(n_x.at[i], nx_s.at[i], nx_r.at[i], at_x(-i - 1))
    n_all[c, y] = (n_zsum[...] + n_x[0]) + (n_x[1] + n_x[2])
    for i, d in enumerate(RING):
        send(n_all.at[c, y], n_all.at[c, y], ny_s.at[i], ny_r.at[i], at_y(d))
    for i in range(4, 7):
        gather_z(gr, g_slot, g_sems, i)
        gather_x(gr, g_slot, g_sems, i - 4)
    for i, d in enumerate(RING):
        arrived(gc.at[c, wrap(y - d, NY)], cy_s.at[i], cy_r.at[i], at_y(-d))
    send(gc.at[c], gc.at[c], cc_s.at[0], cc_r.at[0], at_c)
    for i in range(3, 8):
        gather_x(gr, g_slot, g_sems, i)
    for i, d in enumerate(RING):
        arrived(n_all.at[c, wrap(y - d, NY)], ny_s.at[i], ny_r.at[i], at_y(-d))
    send(n_all.at[c], n_all.at[c], nc_s.at[0], nc_r.at[0], at_c)
    for i in range(8):
        gather_end(gr, g_slot, g_sems, i)
    arrived(gc.at[other], cc_s.at[0], cc_r.at[0], at_c)
    arrived(n_all.at[other], nc_s.at[0], nc_r.at[0], at_c)

    inner = split(n_all[...].reshape(256, 256))
    vt = []
    for half in range(2):
        cols = slice(half * 256, half * 256 + 256)
        mirrored = jnp.concatenate([gc[:, :, :, half * 2 + k].reshape(256, 128) for k in range(2)], axis=1)
        corrected = mirrored - dot3(inner, (zt_hi[:, cols], zt_lo[:, cols]))
        vt.append(dot3(split(t_f32[...]), split(corrected), ((0,), (0,))))
    right_hi, right_lo = split(jnp.concatenate(vt, axis=1))

    writes = []
    for tile in range(8):
        rows = slice(tile * 128, tile * 128 + 128)
        pair = slice(tile % 2 * 2, tile % 2 * 2 + 2)
        g_rows = split(gr[pair, :, :, tile // 2].reshape(256, 128).T)
        update = dot3((yr_hi[rows, :], yr_lo[rows, :]), (right_hi, right_lo))
        update = update + dot3(g_rows, (zt_hi[...], zt_lo[...]))
        for b in range(4):
            at = pl.ds(tile * 512 + b, 128, stride=4)
            out[at, :] = a_f32[at, :] - update[:, b * 128 : b * 128 + 128]
        piece = pl.ds(tile * 512, 512)
        write = pltpu.make_async_copy(out.at[piece], o_hbm.at[piece], o_sem.at[tile])
        write.start()
        writes.append(write)
    for copy in sends:
        copy.wait_send()
    for write in writes:
        write.wait()


def per_device(trailing, reflectors, tfactor):
    flat = trailing.reshape(4096, 128)
    yt = jnp.transpose(reflectors.reshape(4, 2, 128, 8), (0, 1, 3, 2))
    dma = lambda *shape: pltpu.SemaphoreType.DMA(shape)
    vmem = lambda *shape: pltpu.VMEM(shape, F32)
    half = lambda *shape: pltpu.VMEM(shape, BF16)
    result = pl.pallas_call(
        kernel,
        out_shape=jax.ShapeDtypeStruct((4096, 128), F32),
        in_specs=[pl.BlockSpec(memory_space=pl.ANY)] * 3,
        out_specs=pl.BlockSpec(memory_space=pl.ANY),
        scratch_shapes=[
            vmem(4096, 128), half(1024, 512), half(1024, 512), vmem(256, 256), vmem(4096, 128),
            vmem(4, 8, 4, 2, 8, 128), half(256, 1024), half(256, 1024), half(1024, 256), half(1024, 256),
            vmem(4, 8, 4, 8, 128), half(256, 512), half(256, 512), vmem(256, 512),
            vmem(2, 8, 2, 4, 8, 128), vmem(8, 2, 4, 8, 128), vmem(8, 2, 4, 8, 128), vmem(7, 2, 4, 8, 128),
            vmem(2, 8, 2, 4, 8, 128), vmem(4, 8, 2, 4, 8, 128),
            vmem(16, 256), vmem(7, 16, 256), vmem(16, 256), vmem(3, 16, 256), vmem(2, 8, 16, 256),
            dma(3), dma(8),
            dma(7), dma(7), dma(2, 8), dma(2, 8), dma(8), dma(8),
            dma(7), dma(7), dma(2, 8), dma(2, 8), dma(8), dma(8),
            dma(2), dma(2), dma(2, 7), dma(2, 7), dma(2), dma(2),
            dma(1), dma(1), dma(7), dma(7), dma(1), dma(1), dma(7), dma(7), dma(1), dma(1),
            dma(7), dma(7), dma(3), dma(3), dma(7), dma(7), dma(1), dma(1),
        ],
        compiler_params=pltpu.CompilerParams(
            collective_id=0, has_side_effects=True, vmem_limit_bytes=60 * 2**20
        ),
    )(yt, flat, tfactor)
    return result.reshape(trailing.shape)


def solution(mesh):
    return jax.shard_map(
        per_device,
        mesh=mesh,
        in_specs=(P(None, "prow", None, None, "pcol", None), P(None, "prow", None, "pcol"), P()),
        out_specs=P(None, "prow", None, None, "pcol", None),
        check_vma=False,
    )
```

```python
import types

import jax
import jax.numpy as jnp
from jax import lax
from jax.experimental import pallas as pl
from jax.experimental.pallas import tpu as pltpu
from jax.sharding import PartitionSpec as P

F32 = jnp.float32
BF16 = jnp.bfloat16
MESH = pl.DeviceIdType.MESH
NX, NY, NZ, NC = 4, 8, 8, 2
RING = (1, 7, 2, 6, 3, 5, 4)
ONWARD = {2: ((4, 1), (6, 2)), 3: ((5, -1),)}
RELAYED = 4
RELAY_AFTER = {2: (0,), 3: (1,), 5: (2,), 6: (3,)}


def wrap(value, size):
    return lax.rem(value + 2 * size, size)


def device(x, y, z, c):
    return (y * NC + c, x * NZ + z)


def split(value):
    high = value.astype(BF16)
    return high, (value - high.astype(F32)).astype(BF16)


def dot3(left, right, dims=((1,), (0,))):
    def one(a, b):
        return lax.dot_general(a, b, (dims, ((), ())), preferred_element_type=F32)

    return one(left[0], right[0]) + (one(left[0], right[1]) + one(left[1], right[0]))


def in_order(blocks):
    return jnp.concatenate([blocks[:, :, j].reshape(128, blocks.shape[-1]) for j in range(2)], axis=0)


def copy_to(src, dst, send, recv, target):
    return pltpu.make_async_remote_copy(
        src_ref=src, dst_ref=dst, send_sem=send, recv_sem=recv, device_id=target, device_id_type=MESH
    )


def kernel(
    yt_hbm, a_hbm, t_hbm, yr_hi_out, yr_lo_out, vt_hi_out, vt_lo_out, a_out,
    a_f32, a_hi, a_lo, t_f32,
    yr, yr_hi, yr_lo, yc, yc_hi, yc_lo, zt_hi, zt_lo, vt_hi, vt_lo,
    q_part, q_in, q_sum, r_in, gc, gr,
    n_own, n_z, n_zsum, n_x, n_all,
    local, o_sem,
    yz_s, yz_r, yx_s, yx_r, yv_s, yv_r,
    gz_s, gz_r, gx_s, gx_r, gv_s, gv_r,
    c1_s, c1_r, c2_s, c2_r, c3_s, c3_r,
    q_s, q_r, r_s, r_r, p_s, p_r, cy_s, cy_r, cc_s, cc_r,
    nz_s, nz_r, nx_s, nx_r, ny_s, ny_r, nc_s, nc_r,
):
    row, col = lax.axis_index("prow"), lax.axis_index("pcol")
    y, c = lax.div(row, NC), lax.rem(row, NC)
    x, z = lax.div(col, NZ), lax.rem(col, NZ)
    other = 1 - c
    sends, writes = [], []

    def send(src, dst, send_sem, recv_sem, target):
        copy = copy_to(src, dst, send_sem, recv_sem, target)
        copy.start()
        sends.append(copy)

    def arrived(dst, send_sem, recv_sem, target):
        copy_to(dst, dst, send_sem, recv_sem, target).wait_recv()

    def write(src, dst):
        copy = pltpu.make_async_copy(src, dst, o_sem.at[len(writes)])
        copy.start()
        writes.append(copy)

    at_z = lambda d: device(x, y, wrap(z + d, NZ), c)
    at_x = lambda d: device(wrap(x + d, NX), y, z, c)
    at_y = lambda d: device(x, wrap(y + d, NY), z, c)
    at_c = device(x, y, z, other)

    row_x, row_z = lax.div(y, 4), 2 * lax.rem(y, 4) + c
    col_y, col_c = lax.rem(x, 2) * 4 + lax.div(z, 2), lax.rem(z, 2)

    mirror_y = wrap(y + z - row_z + 4, NY)
    mirror_dx = [wrap(x - row_x - 2 * s, NX) for s in range(2)]
    mirror_to = [device(row_x + 2 * s, mirror_y, row_z, lax.rem(mirror_dx[s], 2)) for s in range(2)]
    from_z = wrap(z + y - col_y + 4, NZ)
    from_x = [wrap(x + c + 2 * m, NX) for m in range(2)]
    mirror_from = [device(from_x[m], col_y, from_z, col_c) for m in range(2)]
    piece_to = device(wrap(x + c, NX), col_y, from_z, col_c)
    src_c = wrap(x - row_x, 2)
    src_x = wrap(x - src_c, NX)
    piece_from = device(src_x, mirror_y, row_z, src_c)

    first = lax.rem(x + c, 2)
    kept = (first, 3 - first)
    given = (1 - first, 2 + first)
    j_first = lax.div(wrap(x + first, NX), 2)
    j_at = (j_first, 1 - j_first)

    y_in = pltpu.make_async_copy(yt_hbm, yr.at[x, z], local.at[0])
    a_in = pltpu.make_async_copy(a_hbm, a_f32, local.at[1])
    t_in = pltpu.make_async_copy(t_hbm, t_f32, local.at[2])
    y_in.start()
    barrier = pltpu.get_barrier_semaphore()
    greeted = [at_z(d) for d in RING] + [at_x(d) for d in (1, 2, 3)] + [at_y(d) for d in RING] + [at_c]
    greeted += mirror_to + mirror_from + [piece_to, piece_from]
    for peer in greeted:
        pl.semaphore_signal(barrier, inc=1, device_id=peer, device_id_type=MESH)

    a_in.start()
    t_in.start()
    y_in.wait()
    pl.semaphore_wait(barrier, len(greeted))

    def gather_begin(buf, slot, sems):
        own = buf.at[slot(0, 0)]
        for way, dx in ((0, 1), (1, -1)):
            send(own, own, sems.xs.at[way, 0], sems.xr.at[way, 0], at_x(dx))
        for i in range(4):
            send(own, own, sems.zs.at[i], sems.zr.at[i], at_z(RING[i]))

    def gather_z(buf, slot, sems, i):
        d = RING[i]
        block = buf.at[slot(0, -d)]
        arrived(block, sems.zs.at[i], sems.zr.at[i], at_z(-d))
        for k, dz in ONWARD.get(i, ()):
            send(block, block, sems.zs.at[k], sems.zr.at[k], at_z(dz))
        if i + 1 >= RELAYED:
            send(block, block, sems.vs.at[i + 1], sems.vr.at[i + 1], at_x(2))
        for way, dx in ((0, 1), (1, -1)):
            send(block, block, sems.xs.at[way, i + 1], sems.xr.at[way, i + 1], at_x(dx))

    def gather_x(buf, slot, sems, i, ways=(0, 1)):
        d = (0,) + RING
        for way in ways:
            dx = 1 - 2 * way
            block = buf.at[slot(-dx, -d[i])]
            arrived(block, sems.xs.at[way, i], sems.xr.at[way, i], at_x(-dx))
            if i < RELAYED and i % 2 == way:
                send(block, block, sems.vs.at[i], sems.vr.at[i], at_x(dx))

    def gather_end(buf, slot, sems, i):
        d = (0,) + RING
        dx = 2 if i >= RELAYED else 1 - 2 * (i % 2)
        block = buf.at[slot(2, -d[i])]
        arrived(block, sems.vs.at[i], sems.vr.at[i], at_x(-dx))

    y_sems = types.SimpleNamespace(zs=yz_s, zr=yz_r, xs=yx_s, xr=yx_r, vs=yv_s, vr=yv_r)
    g_sems = types.SimpleNamespace(zs=gz_s, zr=gz_r, xs=gx_s, xr=gx_r, vs=gv_s, vr=gv_r)

    def y_slot(dx, dz):
        return (wrap(x + dx, NX), wrap(z + dz, NZ))

    def g_slot(dx, dz):
        at = wrap(x + dx, NX)
        part = wrap(at - row_x, 2)
        return (lax.div(wrap(at - part, NX), 2), part, wrap(y + z + dz - row_z + 4, NY))

    def multiply(t, dx):
        block = yr.at[wrap(x + dx, NX)]
        parts = [split(block[:, tile // 2, tile % 2].reshape(64, 128)) for tile in range(8)]
        high = jnp.concatenate([part[0] for part in parts], axis=1)
        low = jnp.concatenate([part[1] for part in parts], axis=1)
        both = jnp.concatenate([high, low], axis=0)
        for half in range(2):
            cols = slice(half * 256, half * 256 + 256)
            part = jnp.dot(both, a_hi[:, cols], preferred_element_type=F32)
            part = part[:64] + (part[64:] + jnp.dot(high, a_lo[:, cols], preferred_element_type=F32))
            for k in range(2):
                q_part[t, :, half * 2 + k] = part[:, k * 128 : k * 128 + 128].reshape(8, 8, 128)

    def to_core(h):
        send(q_part.at[given[h]], q_in.at[h], q_s.at[h], q_r.at[h], at_c)

    def scatter(h):
        arrived(q_in.at[h], q_s.at[h], q_r.at[h], at_c)
        for i, d in enumerate(RING):
            to = wrap(y + d, NY)
            q_sum[h, to] = q_part[kept[h], to] + q_in[h, to]
            send(q_sum.at[h, to], r_in.at[h, i], r_s.at[h, i], r_r.at[h, i], at_y(d))

    def collect(h):
        total = q_part[kept[h], y] + q_in[h, y]
        for i, d in enumerate(RING):
            arrived(r_in.at[h, i], r_s.at[h, i], r_r.at[h, i], at_y(-d))
            total = total + r_in[h, i]
        gc[c, y, j_at[h]] = total
        own = gc.at[c, y, j_at[h]]
        send(own, gr.at[lax.div(x, 2), c, y, j_at[h]], p_s.at[h], p_r.at[j_at[h]], piece_to)

    def begin_inner(h):
        left = split(gc[c, y, j_at[h]])
        part = jnp.zeros((8, 256), F32)
        for b in range(4):
            cols = slice(b * 128, b * 128 + 128)
            part = part + dot3((left[0][b], left[1][b]), (yc_hi[:, cols], yc_lo[:, cols]), ((1,), (1,)))
        n_own[h] = part
        for i, d in enumerate(RING):
            send(n_own.at[h], n_z.at[h, i], nz_s.at[h, i], nz_r.at[h, i], at_z(d))

    gather_begin(yr, y_slot, y_sems)
    for s in range(2):
        m = lax.div(mirror_dx[s], 2)
        send(yr.at[x, z, :, s], yc.at[x, z], c1_s.at[s], c1_r.at[m], mirror_to[s])

    def split_a(tiles):
        for tile in tiles:
            for b in range(4):
                high, low = split(a_f32[pl.ds(tile * 512 + b, 128, stride=4), :])
                a_hi[tile * 128 : tile * 128 + 128, b * 128 : b * 128 + 128] = high
                a_lo[tile * 128 : tile * 128 + 128, b * 128 : b * 128 + 128] = low

    def mirror(m):
        block = yc.at[from_x[m], from_z]
        arrived(block, c1_s.at[m], c1_r.at[m], mirror_from[m])
        for i, d in enumerate(RING):
            send(block, block, c2_s.at[m, i], c2_r.at[m, i], at_y(d))

    a_in.wait()
    split_a(range(4))
    for i in range(7):
        gather_z(yr, y_slot, y_sems, i)
        for k in RELAY_AFTER.get(i, ()):
            gather_x(yr, y_slot, y_sems, k)
        if i in (2, 3):
            mirror(i - 2)
    split_a(range(4, 8))
    multiply(0, 0)
    for i in range(RELAYED, 8):
        gather_x(yr, y_slot, y_sems, i, (1,))
    multiply(1, 1)
    to_core(0)
    for i in range(RELAYED, 8):
        gather_x(yr, y_slot, y_sems, i, (0,))
    multiply(2, -1)
    scatter(0)
    for i in range(8):
        gather_end(yr, y_slot, y_sems, i)
    multiply(3, 2)
    to_core(1)
    scatter(1)
    collect(0)
    for m in range(2):
        for i, d in enumerate(RING):
            block = yc.at[from_x[m], wrap(from_z - d, NZ)]
            arrived(block, c2_s.at[m, i], c2_r.at[m, i], at_y(-d))
        send(yc.at[from_x[m]], yc.at[from_x[m]], c3_s.at[m], c3_r.at[m], at_c)
    collect(1)
    for m in range(2):
        block = yc.at[wrap(x + other + 2 * m, NX)]
        arrived(block, c3_s.at[m], c3_r.at[m], at_c)
    for b in range(4):
        high, low = split(yc[:, :, b].reshape(256, 128))
        yc_hi[:, b * 128 : b * 128 + 128] = high
        yc_lo[:, b * 128 : b * 128 + 128] = low
    begin_inner(0)
    begin_inner(1)

    t_in.wait()
    t_parts = split(t_f32[...])
    for half in range(2):
        cols = slice(half * 256, half * 256 + 256)
        high, low = split(dot3(t_parts, (yc_hi[:, cols], yc_lo[:, cols])))
        zt_hi[:, cols] = high
        zt_lo[:, cols] = low
    for tile in range(8):
        high, low = split(yr[:, :, tile // 2, tile % 2].reshape(256, 128).T)
        yr_hi[tile * 128 : tile * 128 + 128, :] = high
        yr_lo[tile * 128 : tile * 128 + 128, :] = low
    write(yr_hi, yr_hi_out)
    write(yr_lo, yr_lo_out)

    own = gc.at[c, y]
    for i, d in enumerate(RING):
        send(own, own, cy_s.at[i], cy_r.at[i], at_y(d))
    own_s, own_k, own_y = g_slot(0, 0)
    for j in range(2):
        arrived(gr.at[own_s, own_k, own_y, j], p_s.at[j], p_r.at[j], piece_from)
    gather_begin(gr, g_slot, g_sems)

    for h in range(2):
        j = j_at[h]
        part = n_own[h]
        for i, d in enumerate(RING):
            arrived(n_z.at[h, i], nz_s.at[h, i], nz_r.at[h, i], at_z(-d))
            part = part + n_z[h, i]
        n_zsum[j] = part
    for i in range(3):
        send(n_zsum, n_x.at[i], nx_s.at[i], nx_r.at[i], at_x(i + 1))

    def gather_g(i):
        gather_z(gr, g_slot, g_sems, i)
        for k in RELAY_AFTER.get(i, ()):
            gather_x(gr, g_slot, g_sems, k)

    for i in range(4):
        gather_g(i)
    for i in range(3):
        arrived(n_x.at[i], nx_s.at[i], nx_r.at[i], at_x(-i - 1))
    n_all[c, y] = (n_zsum[...] + n_x[0]) + (n_x[1] + n_x[2])
    own_n = n_all.at[c, y]
    for i, d in enumerate(RING):
        send(own_n, own_n, ny_s.at[i], ny_r.at[i], at_y(d))
    for i in range(4, 7):
        gather_g(i)

    def subtract(s):
        for b in range(4):
            rows = split(in_order(gr[s, :, :, :, b]).T)
            part = dot3(rows, (zt_hi[...], zt_lo[...]))
            for k in range(4):
                at = pl.ds((2 * b + s) * 512 + k, 128, stride=4)
                a_f32[at, :] = a_f32[at, :] - part[:, k * 128 : k * 128 + 128]

    for i, d in enumerate(RING):
        arrived(gc.at[c, wrap(y - d, NY)], cy_s.at[i], cy_r.at[i], at_y(-d))
    send(gc.at[c], gc.at[c], cc_s.at[0], cc_r.at[0], at_c)
    for i in range(RELAYED, 8):
        gather_x(gr, g_slot, g_sems, i)
    subtract(own_s)
    for i in range(8):
        gather_end(gr, g_slot, g_sems, i)
    for i, d in enumerate(RING):
        arrived(n_all.at[c, wrap(y - d, NY)], ny_s.at[i], ny_r.at[i], at_y(-d))
    send(n_all.at[c], n_all.at[c], nc_s.at[0], nc_r.at[0], at_c)
    subtract(1 - own_s)
    write(a_f32, a_out)
    arrived(gc.at[other], cc_s.at[0], cc_r.at[0], at_c)
    arrived(n_all.at[other], nc_s.at[0], nc_r.at[0], at_c)

    inner = split(in_order(n_all[...]))
    for half in range(2):
        cols = slice(half * 256, half * 256 + 256)
        mirrored = jnp.concatenate([in_order(gc[:, :, :, half * 2 + k]) for k in range(2)], axis=1)
        corrected = mirrored - dot3(inner, (zt_hi[:, cols], zt_lo[:, cols]))
        high, low = split(dot3(t_parts, split(corrected), ((0,), (0,))))
        vt_hi[:, cols] = high
        vt_lo[:, cols] = low
    write(vt_hi, vt_hi_out)
    write(vt_lo, vt_lo_out)
    for copy in sends:
        copy.wait_send()
    for copy in writes:
        copy.wait()


def update(a, yr_hi, yr_lo, vt_hi, vt_lo, out):
    for s in range(4):
        rows = slice(s * 128, s * 128 + 128)
        part = dot3((yr_hi[rows, :], yr_lo[rows, :]), (vt_hi[...], vt_lo[...]))
        for b in range(4):
            at = pl.ds(s * 512 + b, 128, stride=4)
            out[at, :] = a[at, :] - part[:, b * 128 : b * 128 + 128]


def per_device(trailing, reflectors, tfactor):
    flat = trailing.reshape(4096, 128)
    yt = jnp.transpose(reflectors.reshape(4, 2, 128, 8), (0, 1, 3, 2))
    dma = lambda *shape: pltpu.SemaphoreType.DMA(shape)
    vmem = lambda *shape: pltpu.VMEM(shape, F32)
    half = lambda *shape: pltpu.VMEM(shape, BF16)
    out16 = lambda *shape: jax.ShapeDtypeStruct(shape, BF16)
    yr_hi, yr_lo, vt_hi, vt_lo, rest = pl.pallas_call(
        kernel,
        out_shape=[out16(1024, 256)] * 2 + [out16(256, 512)] * 2 + [jax.ShapeDtypeStruct((4096, 128), F32)],
        in_specs=[pl.BlockSpec(memory_space=pl.ANY)] * 3,
        out_specs=[pl.BlockSpec(memory_space=pl.ANY)] * 5,
        scratch_shapes=[
            vmem(4096, 128), half(1024, 512), half(1024, 512), vmem(256, 256),
            vmem(4, 8, 4, 2, 8, 128), half(1024, 256), half(1024, 256),
            vmem(4, 8, 4, 8, 128), *[half(256, 512)] * 6,
            vmem(4, 8, 4, 8, 128), vmem(2, 8, 4, 8, 128), vmem(2, 8, 4, 8, 128), vmem(2, 7, 4, 8, 128),
            vmem(2, 8, 2, 4, 8, 128), vmem(2, 2, 8, 2, 4, 8, 128),
            vmem(2, 8, 256), vmem(2, 7, 8, 256), vmem(2, 8, 256), vmem(3, 2, 8, 256), vmem(2, 8, 2, 8, 256),
            dma(3), dma(5),
            dma(7), dma(7), dma(2, 8), dma(2, 8), dma(8), dma(8),
            dma(7), dma(7), dma(2, 8), dma(2, 8), dma(8), dma(8),
            dma(2), dma(2), dma(2, 7), dma(2, 7), dma(2), dma(2),
            dma(2), dma(2), dma(2, 7), dma(2, 7), dma(2), dma(2), dma(7), dma(7), dma(1), dma(1),
            dma(2, 7), dma(2, 7), dma(3), dma(3), dma(7), dma(7), dma(1), dma(1),
        ],
        compiler_params=pltpu.CompilerParams(
            collective_id=0, has_side_effects=True, vmem_limit_bytes=60 * 2**20
        ),
    )(yt, flat, tfactor)
    whole = pl.BlockSpec((256, 512), lambda b: (0, 0))
    rows = pl.BlockSpec((512, 256), lambda b: (b, 0))
    tiles = pl.BlockSpec((2048, 128), lambda b: (b, 0))
    result = pl.pallas_call(
        update,
        grid=(2,),
        out_shape=jax.ShapeDtypeStruct((4096, 128), F32),
        in_specs=[tiles, rows, rows, whole, whole],
        out_specs=tiles,
        compiler_params=pltpu.CompilerParams(vmem_limit_bytes=60 * 2**20),
    )(rest, yr_hi, yr_lo, vt_hi, vt_lo)
    return result.reshape(trailing.shape)


def solution(mesh):
    return jax.shard_map(
        per_device,
        mesh=mesh,
        in_specs=(P(None, "prow", None, None, "pcol", None), P(None, "prow", None, "pcol"), P()),
        out_specs=P(None, "prow", None, None, "pcol", None),
        check_vma=False,
    )
```

```python
import types

import jax
import jax.numpy as jnp
from jax import lax
from jax.experimental import pallas as pl
from jax.experimental.pallas import tpu as pltpu
from jax.sharding import PartitionSpec as P

F32 = jnp.float32
BF16 = jnp.bfloat16
MESH = pl.DeviceIdType.MESH
NX, NY, NZ, NC = 4, 8, 8, 2
RING = (1, 7, 2, 6, 3, 5, 4)
ONWARD = {2: ((4, 1), (6, 2)), 3: ((5, -1),)}
RELAYED = 4
RELAY_AFTER = {2: (0,), 3: (1,), 5: (2,), 6: (3,)}


def wrap(value, size):
    return lax.rem(value + 2 * size, size)


def device(x, y, z, c):
    return (y * NC + c, x * NZ + z)


def split(value):
    high = value.astype(BF16)
    return high, (value - high.astype(F32)).astype(BF16)


def dot3(left, right, dims=((1,), (0,))):
    def one(a, b):
        return lax.dot_general(a, b, (dims, ((), ())), preferred_element_type=F32)

    return one(left[0], right[0]) + (one(left[0], right[1]) + one(left[1], right[0]))


def in_order(blocks):
    return jnp.concatenate([blocks[:, :, j].reshape(128, blocks.shape[-1]) for j in range(2)], axis=0)


def copy_to(src, dst, send, recv, target):
    return pltpu.make_async_remote_copy(
        src_ref=src, dst_ref=dst, send_sem=send, recv_sem=recv, device_id=target, device_id_type=MESH
    )


def kernel(
    yt_hbm, a_hbm, t_hbm, yr_hi_out, yr_lo_out, vt_hi_out, vt_lo_out, a_out,
    a_f32, a_hi, a_lo, t_f32,
    yr, yr_hi, yr_lo, yc, yc_hi, yc_lo, zt_hi, zt_lo, vt_hi, vt_lo,
    q_part, q_in, q_sum, r_in, gc, gr,
    n_own, n_z, n_zsum, n_x, n_all,
    local, o_sem,
    yz_s, yz_r, yx_s, yx_r, yv_s, yv_r,
    gz_s, gz_r, gx_s, gx_r, gv_s, gv_r,
    c1_s, c1_r, c2_s, c2_r, c3_s, c3_r,
    q_s, q_r, r_s, r_r, p_s, p_r, cy_s, cy_r, cc_s, cc_r,
    nz_s, nz_r, nx_s, nx_r, ny_s, ny_r, nc_s, nc_r,
):
    row, col = lax.axis_index("prow"), lax.axis_index("pcol")
    y, c = lax.div(row, NC), lax.rem(row, NC)
    x, z = lax.div(col, NZ), lax.rem(col, NZ)
    other = 1 - c
    sends, writes = [], []

    def send(src, dst, send_sem, recv_sem, target):
        copy = copy_to(src, dst, send_sem, recv_sem, target)
        copy.start()
        sends.append(copy)

    def drain(count):
        for copy in sends[:count]:
            copy.wait_send()
        del sends[:count]

    def arrived(dst, send_sem, recv_sem, target):
        copy_to(dst, dst, send_sem, recv_sem, target).wait_recv()

    def write(src, dst):
        copy = pltpu.make_async_copy(src, dst, o_sem.at[len(writes)])
        copy.start()
        writes.append(copy)

    at_z = lambda d: device(x, y, wrap(z + d, NZ), c)
    at_x = lambda d: device(wrap(x + d, NX), y, z, c)
    at_y = lambda d: device(x, wrap(y + d, NY), z, c)
    at_c = device(x, y, z, other)

    row_x, row_z = lax.div(y, 4), 2 * lax.rem(y, 4) + c
    col_y, col_c = lax.rem(x, 2) * 4 + lax.div(z, 2), lax.rem(z, 2)

    mirror_y = wrap(y + z - row_z + 4, NY)
    mirror_dx = [wrap(x - row_x - 2 * s, NX) for s in range(2)]
    mirror_to = [device(row_x + 2 * s, mirror_y, row_z, lax.rem(mirror_dx[s], 2)) for s in range(2)]
    from_z = wrap(z + y - col_y + 4, NZ)
    from_x = [wrap(x + c + 2 * m, NX) for m in range(2)]
    mirror_from = [device(from_x[m], col_y, from_z, col_c) for m in range(2)]
    piece_to = device(wrap(x + c, NX), col_y, from_z, col_c)
    src_c = wrap(x - row_x, 2)
    src_x = wrap(x - src_c, NX)
    piece_from = device(src_x, mirror_y, row_z, src_c)

    first = lax.rem(x + c, 2)
    kept = (first, 3 - first)
    given = (1 - first, 2 + first)
    j_first = lax.div(wrap(x + first, NX), 2)
    j_at = (j_first, 1 - j_first)

    y_in = pltpu.make_async_copy(yt_hbm, yr.at[x, z], local.at[0])
    a_in = pltpu.make_async_copy(a_hbm, a_f32, local.at[1])
    t_in = pltpu.make_async_copy(t_hbm, t_f32, local.at[2])
    y_in.start()
    barrier = pltpu.get_barrier_semaphore()
    greeted = [at_z(d) for d in RING] + [at_x(d) for d in (1, 2, 3)] + [at_y(d) for d in RING] + [at_c]
    greeted += mirror_to + mirror_from + [piece_to, piece_from]
    for peer in greeted:
        pl.semaphore_signal(barrier, inc=1, device_id=peer, device_id_type=MESH)

    a_in.start()
    t_in.start()
    y_in.wait()
    pl.semaphore_wait(barrier, len(greeted))

    def gather_begin(buf, slot, sems):
        own = buf.at[slot(0, 0)]
        for way, dx in ((0, 1), (1, -1)):
            send(own, own, sems.xs.at[way, 0], sems.xr.at[way, 0], at_x(dx))
        for i in range(4):
            send(own, own, sems.zs.at[i], sems.zr.at[i], at_z(RING[i]))

    def gather_z(buf, slot, sems, i):
        d = RING[i]
        block = buf.at[slot(0, -d)]
        arrived(block, sems.zs.at[i], sems.zr.at[i], at_z(-d))
        for k, dz in ONWARD.get(i, ()):
            send(block, block, sems.zs.at[k], sems.zr.at[k], at_z(dz))
        if i + 1 >= RELAYED:
            send(block, block, sems.vs.at[i + 1], sems.vr.at[i + 1], at_x(2))
        for way, dx in ((0, 1), (1, -1)):
            send(block, block, sems.xs.at[way, i + 1], sems.xr.at[way, i + 1], at_x(dx))

    def gather_x(buf, slot, sems, i, ways=(0, 1)):
        d = (0,) + RING
        for way in ways:
            dx = 1 - 2 * way
            block = buf.at[slot(-dx, -d[i])]
            arrived(block, sems.xs.at[way, i], sems.xr.at[way, i], at_x(-dx))
            if i < RELAYED and i % 2 == way:
                send(block, block, sems.vs.at[i], sems.vr.at[i], at_x(dx))

    def gather_end(buf, slot, sems, i):
        d = (0,) + RING
        dx = 2 if i >= RELAYED else 1 - 2 * (i % 2)
        block = buf.at[slot(2, -d[i])]
        arrived(block, sems.vs.at[i], sems.vr.at[i], at_x(-dx))

    y_sems = types.SimpleNamespace(zs=yz_s, zr=yz_r, xs=yx_s, xr=yx_r, vs=yv_s, vr=yv_r)
    g_sems = types.SimpleNamespace(zs=gz_s, zr=gz_r, xs=gx_s, xr=gx_r, vs=gv_s, vr=gv_r)

    def y_slot(dx, dz):
        return (wrap(x + dx, NX), wrap(z + dz, NZ))

    def g_slot(dx, dz):
        at = wrap(x + dx, NX)
        part = wrap(at - row_x, 2)
        return (lax.div(wrap(at - part, NX), 2), part, wrap(y + z + dz - row_z + 4, NY))

    def multiply(t, dx):
        block = yr.at[wrap(x + dx, NX)]
        parts = [split(block[:, tile // 2, tile % 2].reshape(64, 128)) for tile in range(8)]
        high = jnp.concatenate([part[0] for part in parts], axis=1)
        low = jnp.concatenate([part[1] for part in parts], axis=1)
        both = jnp.concatenate([high, low], axis=0)
        for half in range(2):
            cols = slice(half * 256, half * 256 + 256)
            part = jnp.dot(both, a_hi[:, cols], preferred_element_type=F32)
            part = part[:64] + (part[64:] + jnp.dot(high, a_lo[:, cols], preferred_element_type=F32))
            for k in range(2):
                q_part[t, :, half * 2 + k] = part[:, k * 128 : k * 128 + 128].reshape(8, 8, 128)

    def to_core(h):
        send(q_part.at[given[h]], q_in.at[h], q_s.at[h], q_r.at[h], at_c)

    def scatter(h):
        arrived(q_in.at[h], q_s.at[h], q_r.at[h], at_c)
        for i, d in enumerate(RING):
            to = wrap(y + d, NY)
            q_sum[h, to] = q_part[kept[h], to] + q_in[h, to]
            send(q_sum.at[h, to], r_in.at[h, i], r_s.at[h, i], r_r.at[h, i], at_y(d))

    def collect(h):
        total = q_part[kept[h], y] + q_in[h, y]
        for i, d in enumerate(RING):
            arrived(r_in.at[h, i], r_s.at[h, i], r_r.at[h, i], at_y(-d))
            total = total + r_in[h, i]
        gc[c, y, j_at[h]] = total
        own = gc.at[c, y, j_at[h]]
        send(own, gr.at[lax.div(x, 2), c, y, j_at[h]], p_s.at[h], p_r.at[j_at[h]], piece_to)

    def begin_inner(h):
        left = split(gc[c, y, j_at[h]])
        part = jnp.zeros((8, 256), F32)
        for b in range(4):
            cols = slice(b * 128, b * 128 + 128)
            part = part + dot3((left[0][b], left[1][b]), (yc_hi[:, cols], yc_lo[:, cols]), ((1,), (1,)))
        n_own[h] = part
        for i, d in enumerate(RING):
            send(n_own.at[h], n_z.at[h, i], nz_s.at[h, i], nz_r.at[h, i], at_z(d))

    gather_begin(yr, y_slot, y_sems)
    for s in range(2):
        m = lax.div(mirror_dx[s], 2)
        send(yr.at[x, z, :, s], yc.at[x, z], c1_s.at[s], c1_r.at[m], mirror_to[s])

    def split_a(tiles):
        for tile in tiles:
            for b in range(4):
                high, low = split(a_f32[pl.ds(tile * 512 + b, 128, stride=4), :])
                a_hi[tile * 128 : tile * 128 + 128, b * 128 : b * 128 + 128] = high
                a_lo[tile * 128 : tile * 128 + 128, b * 128 : b * 128 + 128] = low

    def mirror(m):
        block = yc.at[from_x[m], from_z]
        arrived(block, c1_s.at[m], c1_r.at[m], mirror_from[m])
        for i, d in enumerate(RING):
            send(block, block, c2_s.at[m, i], c2_r.at[m, i], at_y(d))

    a_in.wait()
    split_a(range(4))
    for i in range(7):
        gather_z(yr, y_slot, y_sems, i)
        for k in RELAY_AFTER.get(i, ()):
            gather_x(yr, y_slot, y_sems, k)
        if i in (2, 3):
            mirror(i - 2)
    split_a(range(4, 8))
    multiply(0, 0)
    for i in range(RELAYED, 8):
        gather_x(yr, y_slot, y_sems, i, (1,))
    multiply(1, 1)
    to_core(0)
    for i in range(RELAYED, 8):
        gather_x(yr, y_slot, y_sems, i, (0,))
    multiply(2, -1)
    scatter(0)
    for i in range(8):
        gather_end(yr, y_slot, y_sems, i)
    multiply(3, 2)
    to_core(1)
    started = len(sends)
    scatter(1)
    collect(0)
    for m in range(2):
        for i, d in enumerate(RING):
            block = yc.at[from_x[m], wrap(from_z - d, NZ)]
            arrived(block, c2_s.at[m, i], c2_r.at[m, i], at_y(-d))
        send(yc.at[from_x[m]], yc.at[from_x[m]], c3_s.at[m], c3_r.at[m], at_c)
    for m in range(2):
        block = yc.at[wrap(x + other + 2 * m, NX)]
        arrived(block, c3_s.at[m], c3_r.at[m], at_c)
    for b in range(4):
        high, low = split(yc[:, :, b].reshape(256, 128))
        yc_hi[:, b * 128 : b * 128 + 128] = high
        yc_lo[:, b * 128 : b * 128 + 128] = low
    begin_inner(0)
    drain(started)
    collect(1)
    begin_inner(1)

    t_in.wait()
    t_parts = split(t_f32[...])
    for half in range(2):
        cols = slice(half * 256, half * 256 + 256)
        high, low = split(dot3(t_parts, (yc_hi[:, cols], yc_lo[:, cols])))
        zt_hi[:, cols] = high
        zt_lo[:, cols] = low
    for tile in range(8):
        high, low = split(yr[:, :, tile // 2, tile % 2].reshape(256, 128).T)
        yr_hi[tile * 128 : tile * 128 + 128, :] = high
        yr_lo[tile * 128 : tile * 128 + 128, :] = low
    write(yr_hi, yr_hi_out)
    write(yr_lo, yr_lo_out)

    own = gc.at[c, y]
    for i, d in enumerate(RING):
        send(own, own, cy_s.at[i], cy_r.at[i], at_y(d))
    drain(len(sends) - 7)
    own_s, own_k, own_y = g_slot(0, 0)
    for j in range(2):
        arrived(gr.at[own_s, own_k, own_y, j], p_s.at[j], p_r.at[j], piece_from)
    gather_begin(gr, g_slot, g_sems)

    for h in range(2):
        j = j_at[h]
        part = n_own[h]
        for i, d in enumerate(RING):
            arrived(n_z.at[h, i], nz_s.at[h, i], nz_r.at[h, i], at_z(-d))
            part = part + n_z[h, i]
        n_zsum[j] = part
    for i in range(3):
        send(n_zsum, n_x.at[i], nx_s.at[i], nx_r.at[i], at_x(i + 1))

    def gather_g(i):
        gather_z(gr, g_slot, g_sems, i)
        for k in RELAY_AFTER.get(i, ()):
            gather_x(gr, g_slot, g_sems, k)

    for i in range(4):
        gather_g(i)
    for i in range(3):
        arrived(n_x.at[i], nx_s.at[i], nx_r.at[i], at_x(-i - 1))
    n_all[c, y] = (n_zsum[...] + n_x[0]) + (n_x[1] + n_x[2])
    own_n = n_all.at[c, y]
    for i, d in enumerate(RING):
        send(own_n, own_n, ny_s.at[i], ny_r.at[i], at_y(d))
    for i in range(4, 7):
        gather_g(i)

    def subtract(s):
        for b in range(4):
            rows = split(in_order(gr[s, :, :, :, b]).T)
            part = dot3(rows, (zt_hi[...], zt_lo[...]))
            for k in range(4):
                at = pl.ds((2 * b + s) * 512 + k, 128, stride=4)
                a_f32[at, :] = a_f32[at, :] - part[:, k * 128 : k * 128 + 128]

    for i, d in enumerate(RING):
        arrived(gc.at[c, wrap(y - d, NY)], cy_s.at[i], cy_r.at[i], at_y(-d))
    send(gc.at[c], gc.at[c], cc_s.at[0], cc_r.at[0], at_c)
    for i in range(RELAYED, 8):
        gather_x(gr, g_slot, g_sems, i)
    subtract(own_s)
    for i in range(8):
        gather_end(gr, g_slot, g_sems, i)
    for i, d in enumerate(RING):
        arrived(n_all.at[c, wrap(y - d, NY)], ny_s.at[i], ny_r.at[i], at_y(-d))
    send(n_all.at[c], n_all.at[c], nc_s.at[0], nc_r.at[0], at_c)
    drain(len(sends) - 1)
    subtract(1 - own_s)
    write(a_f32, a_out)
    arrived(gc.at[other], cc_s.at[0], cc_r.at[0], at_c)
    arrived(n_all.at[other], nc_s.at[0], nc_r.at[0], at_c)

    inner = split(in_order(n_all[...]))
    for half in range(2):
        cols = slice(half * 256, half * 256 + 256)
        mirrored = jnp.concatenate([in_order(gc[:, :, :, half * 2 + k]) for k in range(2)], axis=1)
        corrected = mirrored - dot3(inner, (zt_hi[:, cols], zt_lo[:, cols]))
        high, low = split(dot3(t_parts, split(corrected), ((0,), (0,))))
        vt_hi[:, cols] = high
        vt_lo[:, cols] = low
    write(vt_hi, vt_hi_out)
    write(vt_lo, vt_lo_out)
    drain(len(sends))
    for copy in writes:
        copy.wait()


def update(a, yr_hi, yr_lo, vt_hi, vt_lo, out):
    for s in range(4):
        rows = slice(s * 128, s * 128 + 128)
        part = dot3((yr_hi[rows, :], yr_lo[rows, :]), (vt_hi[...], vt_lo[...]))
        for b in range(4):
            at = pl.ds(s * 512 + b, 128, stride=4)
            out[at, :] = a[at, :] - part[:, b * 128 : b * 128 + 128]


def per_device(trailing, reflectors, tfactor):
    flat = trailing.reshape(4096, 128)
    yt = jnp.transpose(reflectors.reshape(4, 2, 128, 8), (0, 1, 3, 2))
    dma = lambda *shape: pltpu.SemaphoreType.DMA(shape)
    vmem = lambda *shape: pltpu.VMEM(shape, F32)
    half = lambda *shape: pltpu.VMEM(shape, BF16)
    out16 = lambda *shape: jax.ShapeDtypeStruct(shape, BF16)
    yr_hi, yr_lo, vt_hi, vt_lo, rest = pl.pallas_call(
        kernel,
        out_shape=[out16(1024, 256)] * 2 + [out16(256, 512)] * 2 + [jax.ShapeDtypeStruct((4096, 128), F32)],
        in_specs=[pl.BlockSpec(memory_space=pl.ANY)] * 3,
        out_specs=[pl.BlockSpec(memory_space=pl.ANY)] * 5,
        scratch_shapes=[
            vmem(4096, 128), half(1024, 512), half(1024, 512), vmem(256, 256),
            vmem(4, 8, 4, 2, 8, 128), half(1024, 256), half(1024, 256),
            vmem(4, 8, 4, 8, 128), *[half(256, 512)] * 6,
            vmem(4, 8, 4, 8, 128), vmem(2, 8, 4, 8, 128), vmem(2, 8, 4, 8, 128), vmem(2, 7, 4, 8, 128),
            vmem(2, 8, 2, 4, 8, 128), vmem(2, 2, 8, 2, 4, 8, 128),
            vmem(2, 8, 256), vmem(2, 7, 8, 256), vmem(2, 8, 256), vmem(3, 2, 8, 256), vmem(2, 8, 2, 8, 256),
            dma(3), dma(5),
            dma(7), dma(7), dma(2, 8), dma(2, 8), dma(8), dma(8),
            dma(7), dma(7), dma(2, 8), dma(2, 8), dma(8), dma(8),
            dma(2), dma(2), dma(2, 7), dma(2, 7), dma(2), dma(2),
            dma(2), dma(2), dma(2, 7), dma(2, 7), dma(2), dma(2), dma(7), dma(7), dma(1), dma(1),
            dma(2, 7), dma(2, 7), dma(3), dma(3), dma(7), dma(7), dma(1), dma(1),
        ],
        compiler_params=pltpu.CompilerParams(
            collective_id=0, has_side_effects=True, vmem_limit_bytes=28 * 2**20
        ),
    )(*[pltpu.with_memory_space_constraint(value, pltpu.HBM) for value in (yt, flat, tfactor)])
    whole = pl.BlockSpec((256, 512), lambda b: (0, 0))
    rows = pl.BlockSpec((512, 256), lambda b: (b, 0))
    tiles = pl.BlockSpec((2048, 128), lambda b: (b, 0))
    result = pl.pallas_call(
        update,
        grid=(2,),
        out_shape=jax.ShapeDtypeStruct((4096, 128), F32),
        in_specs=[tiles, rows, rows, whole, whole],
        out_specs=tiles,
        compiler_params=pltpu.CompilerParams(vmem_limit_bytes=20 * 2**20),
    )(rest, yr_hi, yr_lo, vt_hi, vt_lo)
    return result.reshape(trailing.shape)


def solution(mesh):
    return jax.shard_map(
        per_device,
        mesh=mesh,
        in_specs=(P(None, "prow", None, None, "pcol", None), P(None, "prow", None, "pcol"), P()),
        out_specs=P(None, "prow", None, None, "pcol", None),
        check_vma=False,
    )
```

```python
import types

import jax
import jax.numpy as jnp
from jax import lax
from jax.experimental import pallas as pl
from jax.experimental.pallas import tpu as pltpu
from jax.sharding import PartitionSpec as P

F32 = jnp.float32
BF16 = jnp.bfloat16
MESH = pl.DeviceIdType.MESH
NX, NY, NZ, NC = 4, 8, 8, 2
RING = (1, 7, 2, 6, 3, 5, 4)
ONWARD = {2: ((4, 1), (6, 2)), 3: ((5, -1),)}
RELAYED = 4
RELAY_AFTER = {2: (0,), 3: (1,), 5: (2,), 6: (3,)}


def wrap(value, size):
    return lax.rem(value + 2 * size, size)


def device(x, y, z, c):
    return (y * NC + c, x * NZ + z)


def split(value):
    high = value.astype(BF16)
    return high, (value - high.astype(F32)).astype(BF16)


def dot3(left, right, dims=((1,), (0,))):
    def one(a, b):
        return lax.dot_general(a, b, (dims, ((), ())), preferred_element_type=F32)

    return one(left[0], right[0]) + (one(left[0], right[1]) + one(left[1], right[0]))


def in_order(blocks):
    return jnp.concatenate([blocks[:, :, j].reshape(128, blocks.shape[-1]) for j in range(2)], axis=0)


def copy_to(src, dst, send, recv, target):
    return pltpu.make_async_remote_copy(
        src_ref=src, dst_ref=dst, send_sem=send, recv_sem=recv, device_id=target, device_id_type=MESH
    )


def kernel(
    yt_hbm, a_hbm, t_hbm, yr_hi_out, yr_lo_out, vt_hi_out, vt_lo_out, a_out,
    a_f32, a_hi, a_lo, t_f32,
    yr, yr_hi, yr_lo, yc, yc_hi, yc_lo, zt_hi, zt_lo, vt_hi, vt_lo,
    q_part, q_in, q_sum, r_in, gc, gr,
    n_own, n_z, n_zsum, n_x,
    local, o_sem,
    yz_s, yz_r, yx_s, yx_r, yv_s, yv_r,
    gz_s, gz_r, gx_s, gx_r, gv_s, gv_r,
    c1_s, c1_r, c2_s, c2_r, c3_s, c3_r,
    q_s, q_r, r_s, r_r, p_s, p_r, cy_s, cy_r, cc_s, cc_r,
    nz_s, nz_r, nx_s, nx_r,
):
    row, col = lax.axis_index("prow"), lax.axis_index("pcol")
    y, c = lax.div(row, NC), lax.rem(row, NC)
    x, z = lax.div(col, NZ), lax.rem(col, NZ)
    other = 1 - c
    sends, writes = [], []

    def send(src, dst, send_sem, recv_sem, target):
        copy = copy_to(src, dst, send_sem, recv_sem, target)
        copy.start()
        sends.append(copy)

    def drain(count):
        for copy in sends[:count]:
            copy.wait_send()
        del sends[:count]

    def arrived(dst, send_sem, recv_sem, target):
        copy_to(dst, dst, send_sem, recv_sem, target).wait_recv()

    def write(src, dst):
        copy = pltpu.make_async_copy(src, dst, o_sem.at[len(writes)])
        copy.start()
        writes.append(copy)

    at_z = lambda d: device(x, y, wrap(z + d, NZ), c)
    at_x = lambda d: device(wrap(x + d, NX), y, z, c)
    at_y = lambda d: device(x, wrap(y + d, NY), z, c)
    at_c = device(x, y, z, other)

    row_x, row_z = lax.div(y, 4), 2 * lax.rem(y, 4) + c
    col_y, col_c = lax.rem(x, 2) * 4 + lax.div(z, 2), lax.rem(z, 2)

    mirror_y = wrap(y + z - row_z + 4, NY)
    mirror_dx = [wrap(x - row_x - 2 * s, NX) for s in range(2)]
    mirror_to = [device(row_x + 2 * s, mirror_y, row_z, lax.rem(mirror_dx[s], 2)) for s in range(2)]
    from_z = wrap(z + y - col_y + 4, NZ)
    from_x = [wrap(x + c + 2 * m, NX) for m in range(2)]
    mirror_from = [device(from_x[m], col_y, from_z, col_c) for m in range(2)]
    piece_to = device(wrap(x + c, NX), col_y, from_z, col_c)
    src_c = wrap(x - row_x, 2)
    src_x = wrap(x - src_c, NX)
    piece_from = device(src_x, mirror_y, row_z, src_c)

    first = lax.rem(x + c, 2)
    kept = (first, 3 - first)
    given = (1 - first, 2 + first)
    j_first = lax.div(wrap(x + first, NX), 2)
    j_at = (j_first, 1 - j_first)

    y_in = pltpu.make_async_copy(yt_hbm, yr.at[x, z], local.at[0])
    a_in = pltpu.make_async_copy(a_hbm, a_f32, local.at[1])
    t_in = pltpu.make_async_copy(t_hbm, t_f32, local.at[2])
    y_in.start()
    barrier = pltpu.get_barrier_semaphore()
    greeted = [at_z(d) for d in RING] + [at_x(d) for d in (1, 2, 3)] + [at_y(d) for d in RING] + [at_c]
    greeted += mirror_to + mirror_from + [piece_to, piece_from]
    for peer in greeted:
        pl.semaphore_signal(barrier, inc=1, device_id=peer, device_id_type=MESH)

    a_in.start()
    t_in.start()
    y_in.wait()
    pl.semaphore_wait(barrier, len(greeted))

    def gather_begin(buf, slot, sems):
        own = buf.at[slot(0, 0)]
        for way, dx in ((0, 1), (1, -1)):
            send(own, own, sems.xs.at[way, 0], sems.xr.at[way, 0], at_x(dx))
        for i in range(4):
            send(own, own, sems.zs.at[i], sems.zr.at[i], at_z(RING[i]))

    def gather_z(buf, slot, sems, i):
        d = RING[i]
        block = buf.at[slot(0, -d)]
        arrived(block, sems.zs.at[i], sems.zr.at[i], at_z(-d))
        for k, dz in ONWARD.get(i, ()):
            send(block, block, sems.zs.at[k], sems.zr.at[k], at_z(dz))
        if i + 1 >= RELAYED:
            send(block, block, sems.vs.at[i + 1], sems.vr.at[i + 1], at_x(2))
        for way, dx in ((0, 1), (1, -1)):
            send(block, block, sems.xs.at[way, i + 1], sems.xr.at[way, i + 1], at_x(dx))

    def gather_x(buf, slot, sems, i, ways=(0, 1)):
        d = (0,) + RING
        for way in ways:
            dx = 1 - 2 * way
            block = buf.at[slot(-dx, -d[i])]
            arrived(block, sems.xs.at[way, i], sems.xr.at[way, i], at_x(-dx))
            if i < RELAYED and i % 2 == way:
                send(block, block, sems.vs.at[i], sems.vr.at[i], at_x(dx))

    def gather_end(buf, slot, sems, i):
        d = (0,) + RING
        dx = 2 if i >= RELAYED else 1 - 2 * (i % 2)
        block = buf.at[slot(2, -d[i])]
        arrived(block, sems.vs.at[i], sems.vr.at[i], at_x(-dx))

    y_sems = types.SimpleNamespace(zs=yz_s, zr=yz_r, xs=yx_s, xr=yx_r, vs=yv_s, vr=yv_r)
    g_sems = types.SimpleNamespace(zs=gz_s, zr=gz_r, xs=gx_s, xr=gx_r, vs=gv_s, vr=gv_r)

    def y_slot(dx, dz):
        return (wrap(x + dx, NX), wrap(z + dz, NZ))

    def g_slot(dx, dz):
        at = wrap(x + dx, NX)
        part = wrap(at - row_x, 2)
        return (lax.div(wrap(at - part, NX), 2), part, wrap(y + z + dz - row_z + 4, NY))

    def multiply(t, dx):
        block = yr.at[wrap(x + dx, NX)]
        parts = [split(block[:, tile // 2, tile % 2].reshape(64, 128)) for tile in range(8)]
        high = jnp.concatenate([part[0] for part in parts], axis=1)
        low = jnp.concatenate([part[1] for part in parts], axis=1)
        both = jnp.concatenate([high, low], axis=0)
        for half in range(2):
            cols = slice(half * 256, half * 256 + 256)
            part = jnp.dot(both, a_hi[:, cols], preferred_element_type=F32)
            part = part[:64] + (part[64:] + jnp.dot(high, a_lo[:, cols], preferred_element_type=F32))
            for k in range(2):
                q_part[t, :, half * 2 + k] = part[:, k * 128 : k * 128 + 128].reshape(8, 8, 128)

    def to_core(h):
        send(q_part.at[given[h]], q_in.at[h], q_s.at[h], q_r.at[h], at_c)

    def scatter(h):
        arrived(q_in.at[h], q_s.at[h], q_r.at[h], at_c)
        for i, d in enumerate(RING):
            to = wrap(y + d, NY)
            q_sum[h, to] = q_part[kept[h], to] + q_in[h, to]
            send(q_sum.at[h, to], r_in.at[h, i], r_s.at[h, i], r_r.at[h, i], at_y(d))

    def collect(h):
        total = q_part[kept[h], y] + q_in[h, y]
        for i, d in enumerate(RING):
            arrived(r_in.at[h, i], r_s.at[h, i], r_r.at[h, i], at_y(-d))
            total = total + r_in[h, i]
        gc[c, y, j_at[h]] = total
        own = gc.at[c, y, j_at[h]]
        send(own, gr.at[lax.div(x, 2), c, y, j_at[h]], p_s.at[h], p_r.at[j_at[h]], piece_to)

    def begin_inner(h):
        left = split(gc[c, y, j_at[h]])
        part = jnp.zeros((8, 256), F32)
        for b in range(4):
            cols = slice(b * 128, b * 128 + 128)
            part = part + dot3((left[0][b], left[1][b]), (yc_hi[:, cols], yc_lo[:, cols]), ((1,), (1,)))
        n_own[h] = part
        for i, d in enumerate(RING):
            send(n_own.at[h], n_z.at[h, i], nz_s.at[h, i], nz_r.at[h, i], at_z(d))

    gather_begin(yr, y_slot, y_sems)
    for s in range(2):
        m = lax.div(mirror_dx[s], 2)
        send(yr.at[x, z, :, s], yc.at[x, z], c1_s.at[s], c1_r.at[m], mirror_to[s])

    def split_a(tiles):
        for tile in tiles:
            for b in range(4):
                high, low = split(a_f32[pl.ds(tile * 512 + b, 128, stride=4), :])
                a_hi[tile * 128 : tile * 128 + 128, b * 128 : b * 128 + 128] = high
                a_lo[tile * 128 : tile * 128 + 128, b * 128 : b * 128 + 128] = low

    def mirror(m):
        block = yc.at[from_x[m], from_z]
        arrived(block, c1_s.at[m], c1_r.at[m], mirror_from[m])
        for i, d in enumerate(RING):
            send(block, block, c2_s.at[m, i], c2_r.at[m, i], at_y(d))

    a_in.wait()
    split_a(range(4))
    for i in range(7):
        gather_z(yr, y_slot, y_sems, i)
        for k in RELAY_AFTER.get(i, ()):
            gather_x(yr, y_slot, y_sems, k)
        if i in (2, 3):
            mirror(i - 2)
    split_a(range(4, 8))
    multiply(0, 0)
    for i in range(RELAYED, 8):
        gather_x(yr, y_slot, y_sems, i, (1,))
    multiply(1, 1)
    to_core(0)
    for i in range(RELAYED, 8):
        gather_x(yr, y_slot, y_sems, i, (0,))
    multiply(2, -1)
    scatter(0)
    for i in range(8):
        gather_end(yr, y_slot, y_sems, i)
    multiply(3, 2)
    to_core(1)
    started = len(sends)
    scatter(1)
    collect(0)
    for m in range(2):
        for i, d in enumerate(RING):
            block = yc.at[from_x[m], wrap(from_z - d, NZ)]
            arrived(block, c2_s.at[m, i], c2_r.at[m, i], at_y(-d))
        send(yc.at[from_x[m]], yc.at[from_x[m]], c3_s.at[m], c3_r.at[m], at_c)
    for m in range(2):
        block = yc.at[wrap(x + other + 2 * m, NX)]
        arrived(block, c3_s.at[m], c3_r.at[m], at_c)
    for b in range(4):
        high, low = split(yc[:, :, b].reshape(256, 128))
        yc_hi[:, b * 128 : b * 128 + 128] = high
        yc_lo[:, b * 128 : b * 128 + 128] = low
    begin_inner(0)
    drain(started)
    collect(1)
    begin_inner(1)

    t_in.wait()
    t_parts = split(t_f32[...])
    for half in range(2):
        cols = slice(half * 256, half * 256 + 256)
        high, low = split(dot3(t_parts, (yc_hi[:, cols], yc_lo[:, cols])))
        zt_hi[:, cols] = high
        zt_lo[:, cols] = low
    for tile in range(8):
        high, low = split(yr[:, :, tile // 2, tile % 2].reshape(256, 128).T)
        yr_hi[tile * 128 : tile * 128 + 128, :] = high
        yr_lo[tile * 128 : tile * 128 + 128, :] = low
    write(yr_hi, yr_hi_out)
    write(yr_lo, yr_lo_out)

    drain(len(sends))
    own_s, own_k, own_y = g_slot(0, 0)
    for j in range(2):
        arrived(gr.at[own_s, own_k, own_y, j], p_s.at[j], p_r.at[j], piece_from)
    gather_begin(gr, g_slot, g_sems)

    for h in range(2):
        j = j_at[h]
        part = n_own[h]
        for i, d in enumerate(RING):
            arrived(n_z.at[h, i], nz_s.at[h, i], nz_r.at[h, i], at_z(-d))
            part = part + n_z[h, i]
        n_zsum[j] = part
    for i in range(3):
        send(n_zsum, n_x.at[i], nx_s.at[i], nx_r.at[i], at_x(i + 1))

    def gather_g(i):
        gather_z(gr, g_slot, g_sems, i)
        for k in RELAY_AFTER.get(i, ()):
            gather_x(gr, g_slot, g_sems, k)

    for i in range(4):
        gather_g(i)
    for i in range(3):
        arrived(n_x.at[i], nx_s.at[i], nx_r.at[i], at_x(-i - 1))
    inner = split(((n_zsum[...] + n_x[0]) + (n_x[1] + n_x[2])).reshape(16, 256))
    inner = dot3(inner, (zt_hi[...], zt_lo[...]))
    for b in range(4):
        gc[c, y, :, b] = gc[c, y, :, b] - inner[:, b * 128 : b * 128 + 128].reshape(2, 8, 128)
    own = gc.at[c, y]
    for i, d in enumerate(RING):
        send(own, own, cy_s.at[i], cy_r.at[i], at_y(d))
    for i in range(4, 7):
        gather_g(i)

    def subtract(s):
        for b in range(4):
            rows = split(in_order(gr[s, :, :, :, b]).T)
            part = dot3(rows, (zt_hi[...], zt_lo[...]))
            for k in range(4):
                at = pl.ds((2 * b + s) * 512 + k, 128, stride=4)
                a_f32[at, :] = a_f32[at, :] - part[:, k * 128 : k * 128 + 128]

    for i in range(RELAYED, 8):
        gather_x(gr, g_slot, g_sems, i)
    subtract(own_s)
    for i, d in enumerate(RING):
        arrived(gc.at[c, wrap(y - d, NY)], cy_s.at[i], cy_r.at[i], at_y(-d))
    send(gc.at[c], gc.at[c], cc_s.at[0], cc_r.at[0], at_c)
    for i in range(8):
        gather_end(gr, g_slot, g_sems, i)
    subtract(1 - own_s)
    write(a_f32, a_out)
    arrived(gc.at[other], cc_s.at[0], cc_r.at[0], at_c)
    for half in range(2):
        cols = slice(half * 256, half * 256 + 256)
        corrected = jnp.concatenate([in_order(gc[:, :, :, half * 2 + k]) for k in range(2)], axis=1)
        high, low = split(dot3(t_parts, split(corrected), ((0,), (0,))))
        vt_hi[:, cols] = high
        vt_lo[:, cols] = low
    write(vt_hi, vt_hi_out)
    write(vt_lo, vt_lo_out)
    drain(len(sends))
    for copy in writes:
        copy.wait()


def update(a, yr_hi, yr_lo, vt_hi, vt_lo, out):
    for s in range(4):
        rows = slice(s * 128, s * 128 + 128)
        part = dot3((yr_hi[rows, :], yr_lo[rows, :]), (vt_hi[...], vt_lo[...]))
        for b in range(4):
            at = pl.ds(s * 512 + b, 128, stride=4)
            out[at, :] = a[at, :] - part[:, b * 128 : b * 128 + 128]


def per_device(trailing, reflectors, tfactor):
    flat = trailing.reshape(4096, 128)
    yt = jnp.transpose(reflectors.reshape(4, 2, 128, 8), (0, 1, 3, 2))
    dma = lambda *shape: pltpu.SemaphoreType.DMA(shape)
    vmem = lambda *shape: pltpu.VMEM(shape, F32)
    half = lambda *shape: pltpu.VMEM(shape, BF16)
    out16 = lambda *shape: jax.ShapeDtypeStruct(shape, BF16)
    yr_hi, yr_lo, vt_hi, vt_lo, rest = pl.pallas_call(
        kernel,
        out_shape=[out16(1024, 256)] * 2 + [out16(256, 512)] * 2 + [jax.ShapeDtypeStruct((4096, 128), F32)],
        in_specs=[pl.BlockSpec(memory_space=pl.ANY)] * 3,
        out_specs=[pl.BlockSpec(memory_space=pl.ANY)] * 5,
        scratch_shapes=[
            vmem(4096, 128), half(1024, 512), half(1024, 512), vmem(256, 256),
            vmem(4, 8, 4, 2, 8, 128), half(1024, 256), half(1024, 256),
            vmem(4, 8, 4, 8, 128), *[half(256, 512)] * 6,
            vmem(4, 8, 4, 8, 128), vmem(2, 8, 4, 8, 128), vmem(2, 8, 4, 8, 128), vmem(2, 7, 4, 8, 128),
            vmem(2, 8, 2, 4, 8, 128), vmem(2, 2, 8, 2, 4, 8, 128),
            vmem(2, 8, 256), vmem(2, 7, 8, 256), vmem(2, 8, 256), vmem(3, 2, 8, 256),
            dma(3), dma(5),
            dma(7), dma(7), dma(2, 8), dma(2, 8), dma(8), dma(8),
            dma(7), dma(7), dma(2, 8), dma(2, 8), dma(8), dma(8),
            dma(2), dma(2), dma(2, 7), dma(2, 7), dma(2), dma(2),
            dma(2), dma(2), dma(2, 7), dma(2, 7), dma(2), dma(2), dma(7), dma(7), dma(1), dma(1),
            dma(2, 7), dma(2, 7), dma(3), dma(3),
        ],
        compiler_params=pltpu.CompilerParams(
            collective_id=0, has_side_effects=True, vmem_limit_bytes=28 * 2**20
        ),
    )(*[pltpu.with_memory_space_constraint(value, pltpu.HBM) for value in (yt, flat, tfactor)])
    whole = pl.BlockSpec((256, 512), lambda b: (0, 0))
    rows = pl.BlockSpec((512, 256), lambda b: (b, 0))
    tiles = pl.BlockSpec((2048, 128), lambda b: (b, 0))
    result = pl.pallas_call(
        update,
        grid=(2,),
        out_shape=jax.ShapeDtypeStruct((4096, 128), F32),
        in_specs=[tiles, rows, rows, whole, whole],
        out_specs=tiles,
        compiler_params=pltpu.CompilerParams(vmem_limit_bytes=20 * 2**20),
    )(rest, yr_hi, yr_lo, vt_hi, vt_lo)
    return result.reshape(trailing.shape)


def solution(mesh):
    return jax.shard_map(
        per_device,
        mesh=mesh,
        in_specs=(P(None, "prow", None, None, "pcol", None), P(None, "prow", None, "pcol"), P()),
        out_specs=P(None, "prow", None, None, "pcol", None),
        check_vma=False,
    )
```
